256 devices in a mesh: dom: 32 (over z, y), grp: 8 (over x, core).
Axes of the slice: x: 4, y: 4, z: 8, core: 2. Of those that a mesh axis runs over, the one named last changes fastest.
Arguments:
- deflation: bfloat16 [256, 1024, 3, 2, 128], P(('dom', 'grp')), may hold values from -1.5 to 1.5
- inverse: bfloat16 [256, 2, 1024, 1024], P(('dom', 'grp'))
- operator: bfloat16 [256, 2, 1024, 1024], P(('dom', 'grp'))
- neighbours: int32 [256, 6], P(('dom', 'grp')), may hold values from -1 to 255, as said below
- counts: int32 [256, 6], P(('dom', 'grp')), may hold values from 0 to 256, as said below
- margin_rows: int32 [256, 6, 256], P(('dom', 'grp')), may hold values from 0 to 1023, as said below
- owners: int32 [256, 6, 1], P(('dom', 'grp')), may hold values from 0 to 7; in each aligned block of 6 rows (0 to 5, 6 to 11, ..., all dimensions but the last counted through in order) no two rows name the same one
Outputs:
- owned_blocks: float32 [2048, 3, 2, 128, 128], P(('dom', 'grp'))
The draws below stay inside these ranges and needn't reach their ends.
Inputs may be any that keep to these rules, and one draw needn't show every extreme that they name: `neighbours`: entry n of a subdomain's list is the subdomain with the same group index whose dom index is d + o_n modulo 32 (o_n = -3, -2, -1, 1, 2, 3), or -1 where that pair shares no rows; the relation is symmetric. `counts`: equal on both sides of a pair, 0 exactly where the list holds -1, and 256 for some pair in every draw. `margin_rows`: distinct within each slot; for k below the pair's count, entry k on one side and entry k on the other side name the same global edge. `owners`: among one subdomain's 6 blocks no group index is named more than 1 times; some subdomain names one exactly 1 times.
All inputs are finite; a program needn't handle non-finite values.
Results may differ from the reference program's by a relative error of at most 0.0048.
Values may be sent and summed in bfloat16 or wider, within the bound.
A program may use at most 64 MiB of HBM per device.

```python
import math
import jax
import jax.numpy as jnp
import numpy as np
from jax import lax

EDGES = 1024
K = 128
SETS = 3
MARGIN = 256
SLOTS = 6
SUBS = 256
CAP = 1
N_DOM = 32
N_GRP = 8


OFFSETS = (-3, -2, -1, 1, 2, 3)


def dominant_one(single, real_low, real_high, imag_low, imag_high, real_noise, imag_noise):
    keys = jax.random.split(single, 4)
    factor = EDGES ** (-0.5)
    real_off = jax.random.normal(keys[0], (EDGES, EDGES), jnp.float32)
    imag_off = jax.random.normal(keys[1], (EDGES, EDGES), jnp.float32)
    diag_real = jax.random.uniform(keys[2], (EDGES, 1), jnp.float32, real_low, real_high)
    diag_imag = jax.random.uniform(keys[3], (EDGES, 1), jnp.float32, imag_low, imag_high)
    identity = jnp.eye(EDGES, dtype=jnp.float32)
    real_part = diag_real * identity + real_noise * factor * real_off
    imag_part = diag_imag * identity + imag_noise * factor * imag_off
    return jnp.stack([real_part, imag_part], axis=0).astype(jnp.bfloat16)


def draw_inverse(key, part):
    keys = jax.random.split(jax.random.fold_in(key, 101), SUBS)
    return lax.map(lambda single: dominant_one(single, 0.6, 1.4, -0.3, 0.3, 0.5, 0.3), keys)


def draw_operator(key, part):
    keys = jax.random.split(jax.random.fold_in(key, 202), SUBS)
    return lax.map(lambda single: dominant_one(single, 1.0, 2.0, 0.1, 0.5, 0.6, 0.3), keys)


def pair_tables(key):
    base = jax.random.fold_in(key, 7)
    present = jax.random.randint(jax.random.fold_in(base, 1), (N_DOM, N_GRP, 3), 0, 4) > 0
    drawn = jax.random.randint(jax.random.fold_in(base, 2), (N_DOM, N_GRP, 3), 1, MARGIN + 1)
    present = present.at[0, 0, 0].set(True)
    drawn = drawn.at[0, 0, 0].set(MARGIN)
    present = present.at[:, 0, 2].set(True)
    drawn = drawn.at[0, 0, 2].set(MARGIN)
    dom_index = jnp.arange(N_DOM, dtype=jnp.int32)[:, None]
    grp_index = jnp.arange(N_GRP, dtype=jnp.int32)[None, :]
    neighbour_cols = []
    count_cols = []
    for offset in OFFSETS:
        if offset > 0:
            here = present[:, :, offset - 1]
            sized = drawn[:, :, offset - 1]
        else:
            here = jnp.roll(present[:, :, -offset - 1], -offset, axis=0)
            sized = jnp.roll(drawn[:, :, -offset - 1], -offset, axis=0)
        partner = (dom_index + offset) % N_DOM * N_GRP + grp_index
        neighbour_cols.append(jnp.where(here, partner, -1))
        count_cols.append(jnp.where(here, sized, 0))
    listed = jnp.stack(neighbour_cols, axis=-1).reshape(SUBS, SLOTS).astype(jnp.int32)
    shared = jnp.stack(count_cols, axis=-1).reshape(SUBS, SLOTS).astype(jnp.int32)
    return (listed, shared)


def draw_neighbours(key, part):
    return pair_tables(key)[0]


def draw_counts(key, part):
    return pair_tables(key)[1]


def draw_margin_rows(key, part):
    keys = jax.random.split(jax.random.fold_in(key, 3), SUBS * SLOTS)
    picks = jax.vmap(lambda single: jax.random.permutation(single, EDGES)[:MARGIN])(keys)
    return picks.reshape(SUBS, SLOTS, MARGIN).astype(jnp.int32)


def block_levels(key, extent, cuts, low, high):
    def one(position, parts):
        heights = jax.random.uniform(jax.random.fold_in(jax.random.fold_in(key, 6), position), (parts,), jnp.float32, low / len(cuts), high / len(cuts))
        return jnp.repeat(jnp.exp(heights), extent[position] // parts).reshape((-1,) + (1,) * (len(extent) - position - 1))

    factor_of = one(*cuts[0])
    for cut in cuts[1:]:
        factor_of = factor_of * one(*cut)
    return factor_of


def shared_out(stream_key, own, number, rows, amount, top, bound, slope):
    ranking = jax.random.permutation(stream_key, amount)
    heavy_load, usual = load_shares(amount, rows * top, bound, slope, True), load_shares(amount, rows * top, bound, slope, False)
    places = jnp.arange(amount)

    def named(tallies, rotation):
        used = int((tallies > 0).sum())
        fixed = max(1, used // 4)
        shifted = fixed + (places - fixed + rotation * (used - fixed)) % max(1, amount - fixed)
        return jnp.zeros((amount,), jnp.int32).at[ranking[jnp.where(places < fixed, places, shifted)]].set(jnp.asarray(tallies, jnp.int32))

    tallies = jnp.where(number % 4 == 0, named(heavy_load, number // 4), named(usual, number - number // 4 - 1))
    mixed = jax.random.permutation(jax.random.fold_in(own, 3), amount)
    giver, taker = mixed[0:amount // 2 * 2:2], mixed[1:amount // 2 * 2:2]
    margin = jnp.minimum(tallies[giver] - 1, bound - tallies[taker]) // 2
    margin = jnp.where((giver == ranking[0]) | (taker == ranking[0]) | (tallies[taker] == 0), 0, jnp.maximum(margin, 0))
    shifted = jax.random.randint(jax.random.fold_in(own, 4), (amount // 2,), 0, 1 << 20) % (margin + 1)
    tallies = tallies.at[giver].add(-shifted).at[taker].add(shifted)
    members = jnp.searchsorted(jnp.cumsum(tallies), jnp.arange(rows * top), side="right").astype(jnp.int32)
    listing = members.reshape(top, rows).T
    listing = listing[jax.random.permutation(jax.random.fold_in(own, 1), rows)]
    rotation = jax.random.randint(jax.random.fold_in(own, 2), (rows, 1), 0, top)
    return jnp.take_along_axis(listing, (jnp.arange(top)[None, :] + rotation) % top, axis=1)


def load_shares(amount, total, reach, slope, full):
    weights = [(1 << 20) // math.isqrt(grade ** slope) + 1 for grade in range(1, amount + 1)]
    largest = reach if full else min(reach, max(-(-total // amount), total * weights[0] // sum(weights)))
    least = 1 if total - largest >= amount - 1 else 0
    given, surplus = [largest] + [least] * (amount - 1), total - largest - least * (amount - 1)
    while surplus > 0:
        free = [i for i in range(1, amount) if given[i] < largest] or [i for i in range(1, amount) if given[i] < reach]
        mass, left = sum([weights[i] for i in free]), surplus
        for i in free:
            extra = min(reach - given[i], max(1, left * weights[i] // mass), surplus)
            given[i] = given[i] + extra
            surplus = surplus - extra
    return np.array(given)


def bell_draw(stream_key, shape, deviation, bound, cuts=(), kind=jnp.bfloat16):
    loudness = block_levels(stream_key, shape, cuts, -0.22, 0.18) if cuts else 1.0
    values = jax.random.normal(stream_key, shape, jnp.float32) * deviation * loudness
    return jnp.minimum(jnp.maximum(values, -bound), bound).astype(kind)


def setup_inputs(seed: int = 0) -> dict:
    arg_keys = jax.random.split(jax.random.key(seed), 8)
    deflation = bell_draw(arg_keys[0], (SUBS, EDGES, SETS, 2, K), 0.25, 1.5, ((0, 256),))
    inverse = draw_inverse(jax.random.fold_in(arg_keys[7], 71), 0)
    operator = draw_operator(jax.random.fold_in(arg_keys[7], 71), 0)
    neighbours = draw_neighbours(jax.random.fold_in(arg_keys[7], 71), 0)
    counts = draw_counts(jax.random.fold_in(arg_keys[7], 71), 0)
    margin_rows = draw_margin_rows(jax.random.fold_in(arg_keys[7], 71), 0)
    owners_keys = jax.random.split(jax.random.fold_in(arg_keys[6], 1), SUBS * SLOTS // SLOTS)
    owners_turns = jax.random.permutation(jax.random.fold_in(arg_keys[6], 3), SUBS * SLOTS // SLOTS)
    owners = jax.vmap(lambda own, number: shared_out(jax.random.fold_in(arg_keys[6], 2), own, number, SLOTS, N_GRP, 1, CAP, 2))(owners_keys, owners_turns).reshape((SUBS, SLOTS, 1))
    return dict(deflation=deflation, inverse=inverse, operator=operator, neighbours=neighbours, counts=counts, margin_rows=margin_rows, owners=owners)


OFFSETS = (-3, -2, -1, 1, 2, 3)


def complex_apply(matrix, vectors):
    edges = vectors.shape[0]
    flat = vectors.reshape(edges, -1)
    real_part = jnp.dot(matrix[0], flat, preferred_element_type=jnp.float32).reshape(vectors.shape)
    imag_part = jnp.dot(matrix[1], flat, preferred_element_type=jnp.float32).reshape(vectors.shape)
    result_real = real_part[:, :, 0] - imag_part[:, :, 1]
    result_imag = real_part[:, :, 1] + imag_part[:, :, 0]
    return jnp.stack([result_real, result_imag], axis=2).astype(jnp.bfloat16)


def local_image(inputs):
    inverse_one, operator_one, vectors = inputs
    first = complex_apply(inverse_one, vectors)
    second = complex_apply(inverse_one, first)
    return complex_apply(operator_one, second)


def project_one(inputs):
    projector, arrived = inputs
    shape = projector.shape
    left = projector.reshape(shape[0], shape[1], shape[2], 2 * K).astype(jnp.float32)
    right = arrived.reshape(shape[0], shape[1], shape[2], 2 * K).astype(jnp.float32)
    gram = jnp.einsum("nrsk,nrsl->nskl", left, right, precision=lax.Precision.HIGHEST)
    real_part = gram[:, :, :K, :K] - gram[:, :, K:, K:]
    imag_part = gram[:, :, :K, K:] + gram[:, :, K:, :K]
    return jnp.stack([real_part, imag_part], axis=2)


def take_rows(table, index):
    return table[index]


def reference(deflation, inverse, operator, neighbours, counts, margin_rows, owners):
    vectors = deflation
    images = lax.map(local_image, (inverse, operator, vectors))
    picked = jax.vmap(take_rows)(images, margin_rows)
    positions = jnp.arange(MARGIN, dtype=jnp.int32)
    live = (neighbours[:, :, None] >= 0) & (positions[None, None, :] < counts[:, :, None])
    outgoing = jnp.where(live[..., None, None, None], picked, jnp.zeros((), jnp.bfloat16))
    grid = outgoing.reshape(N_DOM, N_GRP, SLOTS, MARGIN, SETS, 2, K)
    incoming = jnp.stack([jnp.roll(grid[:, :, SLOTS - 1 - index], -OFFSETS[index], axis=0) for index in range(SLOTS)], axis=2)
    incoming = incoming.reshape(SUBS, SLOTS, MARGIN, SETS, 2, K)
    projector = jax.vmap(take_rows)(vectors, margin_rows)
    coupling = lax.map(project_one, (projector, incoming))
    targets = owners[:, :, 0]
    same = targets[:, :, None] == targets[:, None, :]
    slot_ids = jnp.arange(SLOTS, dtype=jnp.int32)
    earlier = slot_ids[None, :] < slot_ids[:, None]
    rank = jnp.sum((same & earlier[None]).astype(jnp.int32), axis=2).astype(jnp.int32)
    place = targets * CAP + rank
    holders = jnp.arange(N_GRP * CAP, dtype=jnp.int32)
    selector = (holders[None, :, None] == place[:, None, :]).astype(jnp.float32)
    routed = jnp.einsum("spn,snwxyz->spwxyz", selector, coupling, precision=lax.Precision.HIGHEST)
    routed = routed.reshape(N_DOM, N_GRP, N_GRP, CAP, SETS, 2, K, K).transpose(0, 2, 1, 3, 4, 5, 6, 7)
    return routed.reshape(SUBS * N_GRP * CAP, SETS, 2, K, K)
```

```python
import functools

import jax
import jax.numpy as jnp
from jax import lax
from jax.experimental import pallas as pl
from jax.experimental.pallas import tpu as pltpu
from jax.sharding import PartitionSpec as P

OFFSETS = (-3, -2, -1, 1, 2, 3)
MESH = pl.DeviceIdType.MESH
F32, BF16 = jnp.float32, jnp.bfloat16


def kernel(
    n_dom, n_grp, sets, width, tile,
    z_hbm, inv_hbm, op_hbm, rows_hbm, nb_ref, cnt_ref, own_ref,
    out_ref,
    zb, zw, inv, op, rows, upright, cols, hot, start, work, image, proj, qs, qr, blocks, rs,
    z_sem, inv_sem, op_sem, rows_sem, qs_sem, qr_sem, rs_sem, rr_sem, own_sem,
):
    slots, margin, edges = hot.shape
    steps = edges // tile
    parts = 2 * sets
    strip = 256
    half = width // 2
    dom, grp = lax.axis_index("dom"), lax.axis_index("grp")

    def matrix_load(source, target, sem, i, part):
        at = pl.multiple_of(i * tile, tile)
        return pltpu.make_async_copy(
            source.at[part, pl.ds(at, tile)],
            target.at[pl.ds(at, tile), pl.ds(part * edges, edges)],
            sem.at[i, part],
        )

    def z_load(i):
        at = pl.multiple_of(i * strip * parts, strip * parts)
        return pltpu.make_async_copy(
            z_hbm.at[pl.ds(at, strip * parts)], zb.at[pl.ds(at, strip * parts)], z_sem.at[i]
        )

    rows_load = pltpu.make_async_copy(rows_hbm, rows, rows_sem)
    rows_load.start()
    for i in range(edges // strip):
        z_load(i).start()

    def load(source, target, sem):
        for i in range(steps):
            for part in range(2):
                matrix_load(source, target, sem, i, part).start()

    load(inv_hbm, inv, inv_sem)

    barrier = pltpu.get_barrier_semaphore()
    for offset in OFFSETS:
        pl.semaphore_signal(
            barrier, inc=1, device_id=(lax.rem(dom + offset + n_dom, n_dom), grp), device_id_type=MESH
        )
    for j in range(1, n_grp):
        pl.semaphore_signal(
            barrier, inc=1, device_id=(dom, lax.rem(grp + j, n_grp)), device_id_type=MESH
        )

    def each(count, body):
        def run(i, carry):
            body(i)
            return carry

        lax.fori_loop(0, count, run, 0)

    def split(q, i, count=tile):
        at = pl.multiple_of(i * count, count)
        real = zw[pl.ds(at * parts + 2 * q, count, stride=parts), :].astype(BF16)
        imag = zw[pl.ds(at * parts + 2 * q + 1, count, stride=parts), :].astype(BF16)
        start[q, pl.ds(at, count), :] = jnp.concatenate([real, imag], axis=1)
        start[q, pl.ds(edges + at, count), :] = jnp.concatenate([-imag, real], axis=1)

    def unpack(i):
        z_load(i).wait()
        at = pl.multiple_of(i * strip * parts, strip * parts)
        zw[pl.ds(at, strip * parts), :] = zb[pl.ds(at, strip * parts), :].astype(F32)
        split(0, i, strip)

    each(edges // strip, unpack)
    load(op_hbm, op, op_sem)

    rows_load.wait()
    upright[...] = jnp.zeros_like(upright)
    for n in range(slots):
        upright[n : n + 1, :] = rows[n]
    cols[...] = jnp.transpose(upright[...])
    part_rows = margin // steps

    def make_hot(i):
        at = pl.multiple_of(i * part_rows, part_rows)
        position = at + lax.broadcasted_iota(jnp.int32, (part_rows, 1), 0)
        lane = lax.broadcasted_iota(jnp.int32, (part_rows, edges), 1)
        for n in range(slots):
            live = jnp.where(nb_ref[0, n] >= 0, cnt_ref[0, n], 0)
            picked = jnp.where(position < live, cols[pl.ds(at, part_rows), n : n + 1], -1)
            hot[n, pl.ds(at, part_rows), :] = jnp.where(lane == picked, 1.0, 0.0).astype(BF16)

    def product(matrix, source, i):
        at = pl.multiple_of(i * tile, tile)
        total = jnp.dot(matrix[pl.ds(at, tile), :], source[...], preferred_element_type=F32)
        rounded = total.astype(BF16)
        return at, rounded[:, :width], rounded[:, width:]

    def apply(matrix, source, target, i):
        at, real, imag = product(matrix, source, i)
        target[pl.ds(at, tile), :] = jnp.concatenate([real, imag], axis=1)
        target[pl.ds(edges + at, tile), :] = jnp.concatenate([-imag, real], axis=1)

    low = lax.broadcasted_iota(jnp.int32, (1, width), 1) < half

    def apply_last(source, i):
        at = pl.multiple_of(i * tile, tile)
        total = jnp.dot(op[pl.ds(at, tile), :], source[...], preferred_element_type=F32)
        real, imag = total[:, :width], total[:, width:]
        image[pl.ds(at, tile), :width] = jnp.where(low, real, pltpu.roll(imag, half, 1)).astype(BF16)
        image[pl.ds(at, tile), width:] = jnp.where(low, pltpu.roll(real, half, 1), imag).astype(BF16)

    pieces = [(q, h) for q in range(sets) for h in (0, 1)]
    ahead = 4

    def rows_out(p, n):
        q, h = pieces[p]
        return pltpu.make_async_remote_copy(
            src_ref=qs.at[q, n, h],
            dst_ref=qr.at[q, slots - 1 - n, h],
            send_sem=qs_sem.at[p, n],
            recv_sem=qr_sem.at[p, slots - 1 - n],
            device_id=(lax.rem(dom + OFFSETS[n] + n_dom, n_dom), grp),
            device_id_type=MESH,
        )

    def block_out(p, j):
        q, h = pieces[p]
        return pltpu.make_async_remote_copy(
            src_ref=rs.at[q, j, h],
            dst_ref=out_ref.at[grp, q, h],
            send_sem=rs_sem.at[p, j],
            recv_sem=rr_sem.at[p, j],
            device_id=(dom, lax.rem(grp + j, n_grp)),
            device_id_type=MESH,
        )

    for q in range(sets):

        def first(i):
            if q == 0:
                matrix_load(inv_hbm, inv, inv_sem, i, 0).wait()
                matrix_load(inv_hbm, inv, inv_sem, i, 1).wait()
                make_hot(i)
            apply(inv, start.at[q], work.at[0], i)

        def second(i):
            if q == 0:
                for other in range(1, sets):
                    split(other, i)
            apply(inv, work.at[0], work.at[1], i)

        def third(i):
            if q == 0:
                matrix_load(op_hbm, op, op_sem, i, 0).wait()
                matrix_load(op_hbm, op, op_sem, i, 1).wait()
            apply_last(work.at[1], i)

        each(steps, first)
        each(steps, second)
        each(steps, third)
        if q == 0:
            pl.semaphore_wait(barrier, slots + n_grp - 1)
        for n in range(slots):
            gathered = jnp.dot(hot[n], image[...], preferred_element_type=F32).astype(BF16)
            qs[q, n, 0] = gathered[:, :width]
            qs[q, n, 1] = gathered[:, width:]
            if 2 * q < ahead:
                rows_out(2 * q, n).start()
        if 2 * q + 1 < ahead:
            for n in range(slots):
                rows_out(2 * q + 1, n).start()

    def project(q, n):
        gathered = jnp.dot(hot[n], start[q, pl.ds(0, edges), :], preferred_element_type=F32)
        proj[q, n] = gathered.astype(BF16)

    for q in range(sets):
        each(slots, functools.partial(project, q))

    blocks[slots] = jnp.zeros(blocks.shape[1:], BF16)
    chosen = []
    for j in range(n_grp):
        there = lax.rem(grp + j, n_grp)
        pick = jnp.int32(slots)
        for n in reversed(range(slots)):
            pick = jnp.where(own_ref[0, n] == there, n, pick)
        chosen.append(pick)

    def couple(q, h, n):
        gram = lax.dot_general(
            proj[q, n], qr[q, n, h], (((0,), (0,)), ((), ())), preferred_element_type=F32
        )
        turned = pltpu.roll(gram[width:], half, 1)
        blocks[n] = (gram[:width] + jnp.where(low, -turned, turned)).astype(BF16)

    def block_kept(q):
        return pltpu.make_async_copy(rs.at[q, 0], out_ref.at[grp, q], own_sem.at[q])

    for p, (q, h) in enumerate(pieces):
        more = p + ahead < len(pieces)
        if more:
            for n in range(slots):
                rows_out(p, slots - 1 - n).wait_recv()
            for n in range(slots):
                rows_out(p + ahead, n).start()
        for n in range(slots):
            if not more:
                rows_out(p, slots - 1 - n).wait_recv()
            couple(q, h, n)
        for j in range(1, n_grp):
            rs[q, j, h] = blocks[chosen[j]]
            block_out(p, j).start()
        rs[q, 0, h] = blocks[chosen[0]]
        if h:
            block_kept(q).start()
    for q in range(sets):
        block_kept(q).wait()
    for p in range(len(pieces)):
        for j in range(1, n_grp):
            block_out(p, j).wait()
        for n in range(slots):
            rows_out(p, n).wait_send()


def widen(packed, out, wide, out_sem):
    count, sets, _, _, width = packed.shape
    half = width // 2
    low = lax.broadcasted_iota(jnp.int32, (1, width), 1) < half

    def store(i):
        return pltpu.make_async_copy(wide.at[i], out.at[i], out_sem.at[i])

    def one_source(i, carry):
        for q in range(sets):
            one, two = packed[i, q, 0].astype(F32), packed[i, q, 1].astype(F32)
            wide[i, q, 0] = jnp.where(low, one, pltpu.roll(two, half, 1))
            wide[i, q, 1] = jnp.where(low, pltpu.roll(one, half, 1), two)
        store(i).start()
        return carry

    lax.fori_loop(0, count, one_source, 0)
    for i in range(count):
        store(i).wait()


def solution(mesh):
    n_dom, n_grp = mesh.shape["dom"], mesh.shape["grp"]

    def on_device(deflation, inverse, operator, neighbours, counts, margin_rows, owners):
        _, edges, sets, _, width = deflation.shape
        slots, margin = margin_rows.shape[1:]
        tile = 512
        steps = edges // tile
        any_space = pl.BlockSpec(memory_space=pl.ANY)
        smem = pl.BlockSpec(memory_space=pltpu.SMEM)
        vmem = pltpu.VMEM
        dma = pltpu.SemaphoreType.DMA
        packed = pl.pallas_call(
            functools.partial(kernel, n_dom, n_grp, sets, width, tile),
            out_shape=pltpu.VMEM((n_grp, sets, 2, width, width), BF16),
            in_specs=[pl.BlockSpec(memory_space=pltpu.HBM)] * 4 + [smem] * 3,
            out_specs=pl.BlockSpec(memory_space=pltpu.VMEM),
            scratch_shapes=[
                vmem((edges * sets * 2, width), BF16),
                vmem((edges * sets * 2, width), F32),
                vmem((edges, 2 * edges), BF16),
                vmem((edges, 2 * edges), BF16),
                vmem((slots, 1, margin), jnp.int32),
                vmem((8, margin), jnp.int32),
                vmem((margin, 8), jnp.int32),
                vmem((slots, margin, edges), BF16),
                vmem((sets, 2 * edges, 2 * width), BF16),
                vmem((2, 2 * edges, 2 * width), BF16),
                vmem((edges, 2 * width), BF16),
                vmem((sets, slots, margin, 2 * width), BF16),
                vmem((sets, slots, 2, margin, width), BF16),
                vmem((sets, slots, 2, margin, width), BF16),
                vmem((slots + 1, width, width), BF16),
                vmem((sets, n_grp, 2, width, width), BF16),
                dma((edges // 256,)),
                dma((steps, 2)),
                dma((steps, 2)),
                dma,
                dma((2 * sets, slots)),
                dma((2 * sets, slots)),
                dma((2 * sets, n_grp)),
                dma((2 * sets, n_grp)),
                dma((sets,)),
            ],
            compiler_params=pltpu.CompilerParams(
                collective_id=0, has_side_effects=True, vmem_limit_bytes=61 * 2**20
            ),
        )(
            deflation.reshape(edges * sets * 2, width),
            inverse[0],
            operator[0],
            margin_rows.reshape(slots, 1, margin),
            neighbours,
            counts,
            owners[:, :, 0],
        )
        return pl.pallas_call(
            widen,
            out_shape=jax.ShapeDtypeStruct(packed.shape, F32),
            in_specs=[pl.BlockSpec(memory_space=pltpu.VMEM)],
            out_specs=any_space,
            scratch_shapes=[vmem(packed.shape, F32), dma((n_grp,))],
            compiler_params=pltpu.CompilerParams(vmem_limit_bytes=16 * 2**20),
        )(packed)

    whole = P(("dom", "grp"))
    return jax.shard_map(
        on_device, mesh=mesh, in_specs=(whole,) * 7, out_specs=whole, check_vma=False
    )
```

```python
import functools

import jax
import jax.numpy as jnp
from jax import lax
from jax.experimental import pallas as pl
from jax.experimental.pallas import tpu as pltpu
from jax.sharding import PartitionSpec as P

OFFSETS = (-3, -2, -1, 1, 2, 3)
SERVED = (1, 4, 0, 5, 2, 3)
MESH = pl.DeviceIdType.MESH
F32, BF16 = jnp.float32, jnp.bfloat16


def kernel(
    n_dom, n_grp, sets, width, tile,
    z_hbm, inv_hbm, op_hbm, rows_hbm, nb_hbm, cnt_hbm, own_hbm,
    out_ref,
    zb, zw, inv, op, rows, upright, cols, hot, start, work, image, proj, qs, qr, blocks, rs,
    nb_ref, cnt_ref, own_ref,
    z_sem, inv_sem, op_sem, rows_sem, small_sem, qs_sem, qr_sem, rs_sem, rr_sem, own_sem,
):
    slots, margin, edges = hot.shape
    steps = edges // tile
    parts = 2 * sets
    strip = 256
    half = width // 2
    dom, grp = lax.axis_index("dom"), lax.axis_index("grp")

    def matrix_load(source, target, sem, i, part):
        at = pl.multiple_of(i * tile, tile)
        return pltpu.make_async_copy(
            source.at[part, pl.ds(at, tile)],
            target.at[pl.ds(at, tile), pl.ds(part * edges, edges)],
            sem.at[i, part],
        )

    def z_load(i):
        at = pl.multiple_of(i * strip * parts, strip * parts)
        return pltpu.make_async_copy(
            z_hbm.at[pl.ds(at, strip * parts)], zb.at[pl.ds(at, strip * parts)], z_sem.at[i]
        )

    rows_load = pltpu.make_async_copy(rows_hbm, rows, rows_sem)
    rows_load.start()
    small = [
        pltpu.make_async_copy(source, target, small_sem.at[i])
        for i, (source, target) in enumerate(((nb_hbm, nb_ref), (cnt_hbm, cnt_ref), (own_hbm, own_ref)))
    ]
    for copy in small:
        copy.start()
    for i in range(edges // strip):
        z_load(i).start()

    def load(source, target, sem):
        for i in range(steps):
            for part in range(2):
                matrix_load(source, target, sem, i, part).start()

    load(inv_hbm, inv, inv_sem)

    barrier = pltpu.get_barrier_semaphore()
    for offset in OFFSETS:
        pl.semaphore_signal(
            barrier, inc=1, device_id=(lax.rem(dom + offset + n_dom, n_dom), grp), device_id_type=MESH
        )
    for j in range(1, n_grp):
        pl.semaphore_signal(
            barrier, inc=1, device_id=(dom, lax.rem(grp + j, n_grp)), device_id_type=MESH
        )

    def each(count, body):
        def run(i, carry):
            body(i)
            return carry

        lax.fori_loop(0, count, run, 0)

    def split(q, i, count=tile):
        at = pl.multiple_of(i * count, count)
        real = zw[pl.ds(at * parts + 2 * q, count, stride=parts), :].astype(BF16)
        imag = zw[pl.ds(at * parts + 2 * q + 1, count, stride=parts), :].astype(BF16)
        start[q, pl.ds(at, count), :] = jnp.concatenate([real, imag], axis=1)
        start[q, pl.ds(edges + at, count), :] = jnp.concatenate([-imag, real], axis=1)

    def unpack(i):
        z_load(i).wait()
        at = pl.multiple_of(i * strip * parts, strip * parts)
        zw[pl.ds(at, strip * parts), :] = zb[pl.ds(at, strip * parts), :].astype(F32)
        split(0, i, strip)

    each(edges // strip, unpack)
    load(op_hbm, op, op_sem)

    rows_load.wait()
    for copy in small:
        copy.wait()
    upright[...] = jnp.zeros_like(upright)
    for n in range(slots):
        upright[n : n + 1, :] = rows[n]
    cols[...] = jnp.transpose(upright[...])
    part_rows = margin // steps

    def make_hot(i):
        at = pl.multiple_of(i * part_rows, part_rows)
        position = at + lax.broadcasted_iota(jnp.int32, (part_rows, 1), 0)
        lane = lax.broadcasted_iota(jnp.int32, (part_rows, edges), 1)
        for n in range(slots):
            live = jnp.where(nb_ref[0, n] >= 0, cnt_ref[0, n], 0)
            picked = jnp.where(position < live, cols[pl.ds(at, part_rows), n : n + 1], -1)
            hot[n, pl.ds(at, part_rows), :] = jnp.where(
                lane.astype(jnp.int16) == picked.astype(jnp.int16), jnp.ones((), BF16), jnp.zeros((), BF16)
            )

    def product(matrix, source, i):
        at = pl.multiple_of(i * tile, tile)
        total = jnp.dot(matrix[pl.ds(at, tile), :], source[...], preferred_element_type=F32)
        rounded = total.astype(BF16)
        return at, rounded[:, :width], rounded[:, width:]

    def apply(matrix, source, target, i):
        at, real, imag = product(matrix, source, i)
        target[pl.ds(at, tile), :] = jnp.concatenate([real, imag], axis=1)
        target[pl.ds(edges + at, tile), :] = jnp.concatenate([-imag, real], axis=1)

    low = lax.broadcasted_iota(jnp.int32, (1, width), 1) < half

    def apply_last(source, i):
        at = pl.multiple_of(i * tile, tile)
        total = jnp.dot(op[pl.ds(at, tile), :], source[...], preferred_element_type=F32)
        real, imag = total[:, :width], total[:, width:]
        image[pl.ds(at, tile), :width] = jnp.where(low, real, pltpu.roll(imag, half, 1)).astype(BF16)
        image[pl.ds(at, tile), width:] = jnp.where(low, pltpu.roll(real, half, 1), imag).astype(BF16)

    pieces = [(q, h) for q in range(sets) for h in (0, 1)]
    ahead = 3

    def rows_out(p, n):
        q, h = pieces[p]
        return pltpu.make_async_remote_copy(
            src_ref=qs.at[q, n, h],
            dst_ref=qr.at[q, slots - 1 - n, h],
            send_sem=qs_sem.at[p, n],
            recv_sem=qr_sem.at[p, slots - 1 - n],
            device_id=(lax.rem(dom + OFFSETS[n] + n_dom, n_dom), grp),
            device_id_type=MESH,
        )

    def block_out(p, j):
        q, h = pieces[p]
        return pltpu.make_async_remote_copy(
            src_ref=rs.at[q, j, h],
            dst_ref=out_ref.at[grp, q, h],
            send_sem=rs_sem.at[p, j],
            recv_sem=rr_sem.at[p, j],
            device_id=(dom, lax.rem(grp + j, n_grp)),
            device_id_type=MESH,
        )

    for q in range(sets):

        def first(i):
            if q == 0:
                matrix_load(inv_hbm, inv, inv_sem, i, 0).wait()
                matrix_load(inv_hbm, inv, inv_sem, i, 1).wait()
                make_hot(i)
            apply(inv, start.at[q], work.at[0], i)

        def second(i):
            if q == 0:
                for other in range(1, sets):
                    split(other, i)
            apply(inv, work.at[0], work.at[1], i)

        def third(i):
            if q == 0:
                matrix_load(op_hbm, op, op_sem, i, 0).wait()
                matrix_load(op_hbm, op, op_sem, i, 1).wait()
            apply_last(work.at[1], i)

        each(steps, first)
        each(steps, second)
        each(steps, third)
        if q == 0:
            pl.semaphore_wait(barrier, slots + n_grp - 1)
        for n in range(slots):
            gathered = jnp.dot(hot[n], image[...], preferred_element_type=F32).astype(BF16)
            qs[q, n, 0] = gathered[:, :width]
            qs[q, n, 1] = gathered[:, width:]
            if 2 * q < ahead:
                rows_out(2 * q, n).start()
        if 2 * q + 1 < ahead:
            for n in range(slots):
                rows_out(2 * q + 1, n).start()

    def project(q, n):
        gathered = jnp.dot(hot[n], start[q, pl.ds(0, edges), :], preferred_element_type=F32)
        proj[q, n] = gathered.astype(BF16)

    blocks[slots] = jnp.zeros(blocks.shape[1:], BF16)
    chosen = []
    for j in range(n_grp):
        there = lax.rem(grp + j, n_grp)
        pick = jnp.int32(slots)
        for n in reversed(range(slots)):
            pick = jnp.where(own_ref[0, n] == there, n, pick)
        chosen.append(pick)

    def couple(q, h, n):
        gram = lax.dot_general(
            proj[q, n], qr[q, n, h], (((0,), (0,)), ((), ())), preferred_element_type=F32
        )
        turned = pltpu.roll(gram[width:], half, 1)
        blocks[n] = (gram[:width] + jnp.where(low, -turned, turned)).astype(BF16)

    def block_kept(q):
        return pltpu.make_async_copy(rs.at[q, 0], out_ref.at[grp, q], own_sem.at[q])

    def settle(p):
        q, h = pieces[p]
        if h:
            block_kept(q).wait()
        for n in range(slots):
            rows_out(p, n).wait_send()
        for j in range(1, n_grp):
            block_out(p, j).wait_send()

    settled = 2
    far_first = sorted(range(1, n_grp), key=lambda j: -min(j, n_grp - j))
    for p, (q, h) in enumerate(pieces):
        if p >= settled:
            settle(p - settled)
        if h == 0:
            each(slots, functools.partial(project, q))
        for n in SERVED:
            rows_out(p, slots - 1 - n).wait_recv()
            if p + ahead < len(pieces):
                rows_out(p + ahead, n).start()
            couple(q, h, n)
        for j in far_first:
            rs[q, j, h] = blocks[chosen[j]]
            block_out(p, j).start()
        rs[q, 0, h] = blocks[chosen[0]]
        if h:
            block_kept(q).start()
    for p in range(len(pieces) - settled, len(pieces)):
        settle(p)
    for p in range(len(pieces)):
        for j in range(1, n_grp):
            block_out(p, j).wait_recv()


def widen(packed, out, wide, out_sem):
    count, sets, _, _, width = packed.shape
    half = width // 2
    low = lax.broadcasted_iota(jnp.int32, (1, width), 1) < half

    def store(i):
        return pltpu.make_async_copy(wide.at[i], out.at[i], out_sem.at[i])

    def one_source(i, carry):
        for q in range(sets):
            one, two = packed[i, q, 0].astype(F32), packed[i, q, 1].astype(F32)
            wide[i, q, 0] = jnp.where(low, one, pltpu.roll(two, half, 1))
            wide[i, q, 1] = jnp.where(low, pltpu.roll(one, half, 1), two)
        store(i).start()
        return carry

    lax.fori_loop(0, count, one_source, 0)
    for i in range(count):
        store(i).wait()


def solution(mesh):
    n_dom, n_grp = mesh.shape["dom"], mesh.shape["grp"]

    def on_device(deflation, inverse, operator, neighbours, counts, margin_rows, owners):
        _, edges, sets, _, width = deflation.shape
        slots, margin = margin_rows.shape[1:]
        tile = 512
        steps = edges // tile
        any_space = pl.BlockSpec(memory_space=pl.ANY)
        vmem = pltpu.VMEM
        dma = pltpu.SemaphoreType.DMA
        packed = pl.pallas_call(
            functools.partial(kernel, n_dom, n_grp, sets, width, tile),
            out_shape=pltpu.VMEM((n_grp, sets, 2, width, width), BF16),
            in_specs=[pl.BlockSpec(memory_space=pltpu.HBM)] * 7,
            out_specs=pl.BlockSpec(memory_space=pltpu.VMEM),
            scratch_shapes=[
                vmem((edges * sets * 2, width), BF16),
                vmem((edges * sets * 2, width), F32),
                vmem((edges, 2 * edges), BF16),
                vmem((edges, 2 * edges), BF16),
                vmem((slots, 1, margin), jnp.int32),
                vmem((8, margin), jnp.int32),
                vmem((margin, 8), jnp.int32),
                vmem((slots, margin, edges), BF16),
                vmem((sets, 2 * edges, 2 * width), BF16),
                vmem((2, 2 * edges, 2 * width), BF16),
                vmem((edges, 2 * width), BF16),
                vmem((sets, slots, margin, 2 * width), BF16),
                vmem((sets, slots, 2, margin, width), BF16),
                vmem((sets, slots, 2, margin, width), BF16),
                vmem((slots + 1, width, width), BF16),
                vmem((sets, n_grp, 2, width, width), BF16),
                pltpu.SMEM((1, slots), jnp.int32),
                pltpu.SMEM((1, slots), jnp.int32),
                pltpu.SMEM((1, slots), jnp.int32),
                dma((edges // 256,)),
                dma((steps, 2)),
                dma((steps, 2)),
                dma,
                dma((3,)),
                dma((2 * sets, slots)),
                dma((2 * sets, slots)),
                dma((2 * sets, n_grp)),
                dma((2 * sets, n_grp)),
                dma((sets,)),
            ],
            compiler_params=pltpu.CompilerParams(
                collective_id=0, has_side_effects=True, vmem_limit_bytes=61 * 2**20
            ),
        )(
            deflation.reshape(edges * sets * 2, width),
            inverse[0],
            operator[0],
            margin_rows.reshape(slots, 1, margin),
            neighbours,
            counts,
            owners[:, :, 0],
        )
        return pl.pallas_call(
            widen,
            out_shape=jax.ShapeDtypeStruct(packed.shape, F32),
            in_specs=[pl.BlockSpec(memory_space=pltpu.VMEM)],
            out_specs=any_space,
            scratch_shapes=[vmem(packed.shape, F32), dma((n_grp,))],
            compiler_params=pltpu.CompilerParams(vmem_limit_bytes=16 * 2**20),
        )(packed)

    whole = P(("dom", "grp"))
    return jax.shard_map(
        on_device, mesh=mesh, in_specs=(whole,) * 7, out_specs=whole, check_vma=False
    )
```

```python
import functools

import jax
import jax.numpy as jnp
from jax import lax
from jax.experimental import pallas as pl
from jax.experimental.pallas import tpu as pltpu
from jax.sharding import PartitionSpec as P

OFFSETS = (-3, -2, -1, 1, 2, 3)
SERVED = (1, 4, 0, 5, 2, 3)
MESH = pl.DeviceIdType.MESH
F32, BF16 = jnp.float32, jnp.bfloat16


def kernel(
    n_dom, n_grp, sets, width, tile,
    z_hbm, inv_hbm, op_hbm, rows_hbm, nb_hbm, cnt_hbm, own_hbm,
    out_ref,
    zb, zw, inv, op, rows, upright, cols, hot, start, work, image, proj, qs, qr, blocks, rs,
    nb_ref, cnt_ref, own_ref,
    z_sem, inv_sem, op_sem, rows_sem, small_sem, qs_sem, qr_sem, rs_sem, rr_sem, own_sem,
):
    slots, margin, edges = hot.shape
    steps = edges // tile
    parts = 2 * sets
    strip = 256
    half = width // 2
    dom, grp = lax.axis_index("dom"), lax.axis_index("grp")

    def matrix_load(source, target, sem, i, part):
        at = pl.multiple_of(i * tile, tile)
        return pltpu.make_async_copy(
            source.at[part, pl.ds(at, tile)],
            target.at[pl.ds(at, tile), pl.ds(part * edges, edges)],
            sem.at[i, part],
        )

    def z_load(i):
        at = pl.multiple_of(i * strip * parts, strip * parts)
        return pltpu.make_async_copy(
            z_hbm.at[pl.ds(at, strip * parts)], zb.at[pl.ds(at, strip * parts)], z_sem.at[i]
        )

    rows_load = pltpu.make_async_copy(rows_hbm, rows, rows_sem)
    rows_load.start()
    small = [
        pltpu.make_async_copy(source, target, small_sem.at[i])
        for i, (source, target) in enumerate(((nb_hbm, nb_ref), (cnt_hbm, cnt_ref), (own_hbm, own_ref)))
    ]
    for copy in small:
        copy.start()
    for i in range(edges // strip):
        z_load(i).start()

    def load(source, target, sem):
        for i in range(steps):
            for part in range(2):
                matrix_load(source, target, sem, i, part).start()

    load(inv_hbm, inv, inv_sem)

    barrier = pltpu.get_barrier_semaphore()
    for offset in OFFSETS:
        pl.semaphore_signal(
            barrier, inc=1, device_id=(lax.rem(dom + offset + n_dom, n_dom), grp), device_id_type=MESH
        )
    for j in range(1, n_grp):
        pl.semaphore_signal(
            barrier, inc=1, device_id=(dom, lax.rem(grp + j, n_grp)), device_id_type=MESH
        )

    def each(count, body):
        def run(i, carry):
            body(i)
            return carry

        lax.fori_loop(0, count, run, 0)

    def split(q, i, count=tile):
        at = pl.multiple_of(i * count, count)
        real = zw[pl.ds(at * parts + 2 * q, count, stride=parts), :].astype(BF16)
        imag = zw[pl.ds(at * parts + 2 * q + 1, count, stride=parts), :].astype(BF16)
        start[q, pl.ds(at, count), :] = jnp.concatenate([real, imag], axis=1)
        start[q, pl.ds(edges + at, count), :] = jnp.concatenate([-imag, real], axis=1)

    def unpack(i):
        z_load(i).wait()
        at = pl.multiple_of(i * strip * parts, strip * parts)
        zw[pl.ds(at, strip * parts), :] = zb[pl.ds(at, strip * parts), :].astype(F32)
        split(0, i, strip)

    each(edges // strip, unpack)
    load(op_hbm, op, op_sem)

    rows_load.wait()
    for copy in small:
        copy.wait()
    upright[...] = jnp.zeros_like(upright)
    for n in range(slots):
        upright[n : n + 1, :] = rows[n]
    cols[...] = jnp.transpose(upright[...])
    part_rows = margin // steps

    def make_hot(i):
        at = pl.multiple_of(i * part_rows, part_rows)
        position = at + lax.broadcasted_iota(jnp.int32, (part_rows, 1), 0)
        lane = lax.broadcasted_iota(jnp.int32, (part_rows, edges), 1)
        for n in range(slots):
            live = jnp.where(nb_ref[0, n] >= 0, cnt_ref[0, n], 0)
            picked = jnp.where(position < live, cols[pl.ds(at, part_rows), n : n + 1], -1)
            hot[n, pl.ds(at, part_rows), :] = jnp.where(
                lane.astype(jnp.int16) == picked.astype(jnp.int16), jnp.ones((), BF16), jnp.zeros((), BF16)
            )

    def product(matrix, source, i):
        at = pl.multiple_of(i * tile, tile)
        total = jnp.dot(matrix[pl.ds(at, tile), :], source[...], preferred_element_type=F32)
        rounded = total.astype(BF16)
        return at, rounded[:, :width], rounded[:, width:]

    def apply(matrix, source, target, i):
        at, real, imag = product(matrix, source, i)
        target[pl.ds(at, tile), :] = jnp.concatenate([real, imag], axis=1)
        target[pl.ds(edges + at, tile), :] = jnp.concatenate([-imag, real], axis=1)

    low = lax.broadcasted_iota(jnp.int32, (1, width), 1) < half

    def apply_last(source, i):
        at = pl.multiple_of(i * tile, tile)
        total = jnp.dot(op[pl.ds(at, tile), :], source[...], preferred_element_type=F32)
        real, imag = total[:, :width], total[:, width:]
        image[pl.ds(at, tile), :width] = jnp.where(low, real, pltpu.roll(imag, half, 1)).astype(BF16)
        image[pl.ds(at, tile), width:] = jnp.where(low, pltpu.roll(real, half, 1), imag).astype(BF16)

    pieces = [(q, h) for q in range(sets) for h in (0, 1)]
    ahead = 3

    def rows_out(p, n):
        q, h = pieces[p]
        return pltpu.make_async_remote_copy(
            src_ref=qs.at[q, n, h],
            dst_ref=qr.at[q, slots - 1 - n, h],
            send_sem=qs_sem.at[p, n],
            recv_sem=qr_sem.at[p, slots - 1 - n],
            device_id=(lax.rem(dom + OFFSETS[n] + n_dom, n_dom), grp),
            device_id_type=MESH,
        )

    def block_out(p, j):
        q, h = pieces[p]
        return pltpu.make_async_remote_copy(
            src_ref=rs.at[q, j, h],
            dst_ref=out_ref.at[grp, q, h],
            send_sem=rs_sem.at[p, j],
            recv_sem=rr_sem.at[p, j],
            device_id=(dom, lax.rem(grp + j, n_grp)),
            device_id_type=MESH,
        )

    for q in range(sets):

        def first(i):
            if q == 0:
                matrix_load(inv_hbm, inv, inv_sem, i, 0).wait()
                matrix_load(inv_hbm, inv, inv_sem, i, 1).wait()
                make_hot(i)
            apply(inv, start.at[q], work.at[0], i)

        def second(i):
            if q == 0:
                for other in range(1, sets):
                    split(other, i)
            apply(inv, work.at[0], work.at[1], i)

        def third(i):
            if q == 0:
                matrix_load(op_hbm, op, op_sem, i, 0).wait()
                matrix_load(op_hbm, op, op_sem, i, 1).wait()
            apply_last(work.at[1], i)

        each(steps, first)
        each(steps, second)
        each(steps, third)
        if q == 0:
            pl.semaphore_wait(barrier, slots + n_grp - 1)
        for n in SERVED:
            gathered = jnp.dot(hot[n], image[...], preferred_element_type=F32).astype(BF16)
            qs[q, n, 0] = gathered[:, :width]
            qs[q, n, 1] = gathered[:, width:]
            if 2 * q < ahead:
                rows_out(2 * q, n).start()
        if 2 * q + 1 < ahead:
            for n in SERVED:
                rows_out(2 * q + 1, n).start()

    def project(q, n):
        gathered = jnp.dot(hot[n], start[q, pl.ds(0, edges), :], preferred_element_type=F32)
        proj[q, n] = gathered.astype(BF16)

    blocks[slots] = jnp.zeros(blocks.shape[1:], BF16)
    chosen = []
    for j in range(n_grp):
        there = lax.rem(grp + j, n_grp)
        pick = jnp.int32(slots)
        for n in reversed(range(slots)):
            pick = jnp.where(own_ref[0, n] == there, n, pick)
        chosen.append(pick)

    def couple(q, h, n):
        gram = lax.dot_general(
            proj[q, n], qr[q, n, h], (((0,), (0,)), ((), ())), preferred_element_type=F32
        )
        turned = pltpu.roll(gram[width:], half, 1)
        blocks[n] = (gram[:width] + jnp.where(low, -turned, turned)).astype(BF16)

    def block_kept(q):
        return pltpu.make_async_copy(rs.at[q, 0], out_ref.at[grp, q], own_sem.at[q])

    def settle(p):
        q, h = pieces[p]
        if h:
            block_kept(q).wait()
        for n in range(slots):
            rows_out(p, n).wait_send()
        for j in range(1, n_grp):
            block_out(p, j).wait_send()

    settled = 2
    far_first = sorted(range(1, n_grp), key=lambda j: -min(j, n_grp - j))
    for p, (q, h) in enumerate(pieces):
        if p >= settled:
            settle(p - settled)
        if h == 0:
            each(slots, functools.partial(project, q))
        for n in SERVED:
            rows_out(p, slots - 1 - n).wait_recv()
            if p + ahead < len(pieces):
                rows_out(p + ahead, n).start()
            couple(q, h, n)
        for j in far_first:
            rs[q, j, h] = blocks[chosen[j]]
            block_out(p, j).start()
        rs[q, 0, h] = blocks[chosen[0]]
        if h:
            block_kept(q).start()
    for p in range(len(pieces) - settled, len(pieces)):
        settle(p)
    for p in range(len(pieces)):
        for j in range(1, n_grp):
            block_out(p, j).wait_recv()


def widen(packed, out, wide, out_sem):
    count, sets, _, _, width = packed.shape
    half = width // 2
    low = lax.broadcasted_iota(jnp.int32, (1, width), 1) < half

    def store(i):
        return pltpu.make_async_copy(wide.at[i], out.at[i], out_sem.at[i])

    def one_source(i, carry):
        for q in range(sets):
            one, two = packed[i, q, 0].astype(F32), packed[i, q, 1].astype(F32)
            wide[i, q, 0] = jnp.where(low, one, pltpu.roll(two, half, 1))
            wide[i, q, 1] = jnp.where(low, pltpu.roll(one, half, 1), two)
        store(i).start()
        return carry

    lax.fori_loop(0, count, one_source, 0)
    for i in range(count):
        store(i).wait()


def solution(mesh):
    n_dom, n_grp = mesh.shape["dom"], mesh.shape["grp"]

    def on_device(deflation, inverse, operator, neighbours, counts, margin_rows, owners):
        _, edges, sets, _, width = deflation.shape
        slots, margin = margin_rows.shape[1:]
        tile = 512
        steps = edges // tile
        any_space = pl.BlockSpec(memory_space=pl.ANY)
        vmem = pltpu.VMEM
        dma = pltpu.SemaphoreType.DMA
        packed = pl.pallas_call(
            functools.partial(kernel, n_dom, n_grp, sets, width, tile),
            out_shape=pltpu.VMEM((n_grp, sets, 2, width, width), BF16),
            in_specs=[pl.BlockSpec(memory_space=pltpu.HBM)] * 7,
            out_specs=pl.BlockSpec(memory_space=pltpu.VMEM),
            scratch_shapes=[
                vmem((edges * sets * 2, width), BF16),
                vmem((edges * sets * 2, width), F32),
                vmem((edges, 2 * edges), BF16),
                vmem((edges, 2 * edges), BF16),
                vmem((slots, 1, margin), jnp.int32),
                vmem((8, margin), jnp.int32),
                vmem((margin, 8), jnp.int32),
                vmem((slots, margin, edges), BF16),
                vmem((sets, 2 * edges, 2 * width), BF16),
                vmem((2, 2 * edges, 2 * width), BF16),
                vmem((edges, 2 * width), BF16),
                vmem((sets, slots, margin, 2 * width), BF16),
                vmem((sets, slots, 2, margin, width), BF16),
                vmem((sets, slots, 2, margin, width), BF16),
                vmem((slots + 1, width, width), BF16),
                vmem((sets, n_grp, 2, width, width), BF16),
                pltpu.SMEM((1, slots), jnp.int32),
                pltpu.SMEM((1, slots), jnp.int32),
                pltpu.SMEM((1, slots), jnp.int32),
                dma((edges // 256,)),
                dma((steps, 2)),
                dma((steps, 2)),
                dma,
                dma((3,)),
                dma((2 * sets, slots)),
                dma((2 * sets, slots)),
                dma((2 * sets, n_grp)),
                dma((2 * sets, n_grp)),
                dma((sets,)),
            ],
            compiler_params=pltpu.CompilerParams(
                collective_id=0, has_side_effects=True, vmem_limit_bytes=61 * 2**20
            ),
        )(
            deflation.reshape(edges * sets * 2, width),
            inverse[0],
            operator[0],
            margin_rows.reshape(slots, 1, margin),
            neighbours,
            counts,
            owners[:, :, 0],
        )
        return pl.pallas_call(
            widen,
            out_shape=jax.ShapeDtypeStruct(packed.shape, F32),
            in_specs=[pl.BlockSpec(memory_space=pltpu.VMEM)],
            out_specs=any_space,
            scratch_shapes=[vmem(packed.shape, F32), dma((n_grp,))],
            compiler_params=pltpu.CompilerParams(vmem_limit_bytes=16 * 2**20),
        )(packed)

    whole = P(("dom", "grp"))
    return jax.shard_map(
        on_device, mesh=mesh, in_specs=(whole,) * 7, out_specs=whole, check_vma=False
    )
```
